1024 devices in a mesh: dp: 64 (over z_lo, y), expert: 16 (over x, z_hi, core).
Axes of the slice: x: 4, y: 4, z: 32 (z_hi: 2, z_lo: 16; z = z_hi * 16 + z_lo), core: 2. Of those that a mesh axis runs over, the one named last changes fastest.
Arguments:
- tokens: bfloat16 [131072, 1024], P(('dp', 'expert')), may hold values from -6 to 6
- norm_gain: float32 [1024], replicated, may hold values from 0.25 to 1.75
- router_w: bfloat16 [1024, 16], replicated, may hold values from -0.1875 to 0.1875
- w_gate: bfloat16 [16, 1024, 384], P('expert'), may hold values from -0.1875 to 0.1875
- w_up: bfloat16 [16, 1024, 384], P('expert'), may hold values from -0.1875 to 0.1875
- w_down: bfloat16 [16, 384, 1024], P('expert'), may hold values from -0.3125 to 0.3125
- routes: int32 [131072, 2], P(('dp', 'expert')), may hold values from 0 to 15, all different within a row; in each aligned block of 128 rows (0 to 127, 128 to 255, ...) at most 24 rows name the same one
- grad_out: bfloat16 [131072, 1024], P(('dp', 'expert')), may hold values from -24 to 24
Outputs:
- layer_out: bfloat16 [131072, 1024], P(('dp', 'expert'))
- d_tokens: bfloat16 [131072, 1024], P(('dp', 'expert'))
- d_gain: float32 [1024], replicated
- d_router: float32 [1024, 16], replicated
- d_gate_w: float32 [16, 1024, 384], P('expert', 'dp')
- d_up_w: float32 [16, 1024, 384], P('expert', 'dp')
- d_down_w: float32 [16, 384, 1024], P('expert', None, 'dp')
The draws below stay inside these ranges and needn't reach their ends.
Inputs may be any that keep to these rules, and one draw needn't show every extreme that they name: `routes`: each row names 2 different experts. In each aligned block of 128 rows (the rows of one device) no expert is named by more than 24 rows, a bound that some block reaches.
All inputs are finite; a program needn't handle non-finite values.
Results may differ from the reference program's by a relative error of at most 0.0073.
Values may be sent and summed in bfloat16 or wider, within the bound.
A program may use at most 64 MiB of HBM per device.

```python
import math
import jax
import jax.numpy as jnp
import numpy as np
from jax import lax

D = 1024
FF = 384
TOK_DEV = 128
TOP = 2
EXPERTS = 16
TOKENS = 131072
MOST = 24
N_DP = 64
N_EXPERT = 16


def with_spikes(values, rng, source, target, blocks, factor):
    def block_of(dim):
        return (jnp.arange(values.shape[dim]) // (values.shape[dim] // blocks)).reshape((-1,) + (1,) * (values.ndim - 1 - dim))

    first = jax.random.permutation(rng, blocks)[block_of(target)]
    far = (block_of(target) + blocks // 2) % blocks
    return jnp.where((block_of(source) == first) | (block_of(source) == far), factor * values, values)


def levels(stream_key, extent, cuts, least, top_value):
    loudness = 1.0
    for position, parts in cuts:
        draws = jax.random.uniform(jax.random.fold_in(jax.random.fold_in(stream_key, 6), position), (parts,), jnp.float32, least / len(cuts), top_value / len(cuts))
        loudness = loudness * jnp.repeat(jnp.exp(draws), extent[position] // parts).reshape((-1,) + (1,) * (len(extent) - 1 - position))
    return loudness


def shared_out(key, own, number, rows, count, top, limit, slope):
    order = jax.random.permutation(key, count)
    packed, ordinary = portions_of(count, rows * top, limit, slope, True), portions_of(count, rows * top, limit, slope, False)
    places = jnp.arange(count)

    def named(lengths, turn):
        used = int((lengths > 0).sum())
        fixed = max(1, used // 4)
        moved = fixed + (places - fixed + turn * (used - fixed)) % max(1, count - fixed)
        return jnp.zeros((count,), jnp.int32).at[order[jnp.where(places < fixed, places, moved)]].set(jnp.asarray(lengths, jnp.int32))

    lengths = jnp.where(number % 4 == 0, named(packed, number // 4), named(ordinary, number - number // 4 - 1))
    mixed = jax.random.permutation(jax.random.fold_in(own, 3), count)
    source_of, receiver = mixed[0:count // 2 * 2:2], mixed[1:count // 2 * 2:2]
    margin = jnp.minimum(lengths[source_of] - 1, limit - lengths[receiver]) // 2
    margin = jnp.where((source_of == order[0]) | (receiver == order[0]) | (lengths[receiver] == 0), 0, jnp.maximum(margin, 0))
    moved = jax.random.randint(jax.random.fold_in(own, 4), (count // 2,), 0, 1 << 20) % (margin + 1)
    lengths = lengths.at[source_of].add(-moved).at[receiver].add(moved)
    members = jnp.searchsorted(jnp.cumsum(lengths), jnp.arange(rows * top), side="right").astype(jnp.int32)
    grid = members.reshape(top, rows).T
    grid = grid[jax.random.permutation(jax.random.fold_in(own, 1), rows)]
    turn = jax.random.randint(jax.random.fold_in(own, 2), (rows, 1), 0, top)
    return jnp.take_along_axis(grid, (jnp.arange(top)[None, :] + turn) % top, axis=1)


def portions_of(number_of, total, limit, slope, full):
    portions = [(1 << 20) // math.isqrt(rank ** slope) + 1 for rank in range(1, number_of + 1)]
    largest = limit if full else min(limit, max(-(-total // number_of), total * portions[0] // sum(portions)))
    least = 1 if total - largest >= number_of - 1 else 0
    counts, rest = [largest] + [least] * (number_of - 1), total - largest - least * (number_of - 1)
    while rest > 0:
        free = [i for i in range(1, number_of) if counts[i] < largest] or [i for i in range(1, number_of) if counts[i] < limit]
        whole, budget = sum([portions[i] for i in free]), rest
        for i in free:
            more = min(limit - counts[i], max(1, budget * portions[i] // whole), rest)
            counts[i] = counts[i] + more
            rest = rest - more
    return np.array(counts)


def bell_draw(key, extent, spread, bound, cuts=(), kind=jnp.bfloat16):
    drawn = spread * jax.random.normal(key, extent, jnp.float32)
    if cuts:
        drawn = drawn * levels(key, extent, cuts, -0.22, 0.18)
    return jnp.clip(drawn, -bound, bound).astype(kind)


def bell_draw_with(own_key, dims, deviation, most, cuts, heavy, held_as=jnp.bfloat16):
    drawn = deviation * jax.random.normal(own_key, dims, jnp.float32)
    if cuts:
        drawn = drawn * levels(own_key, dims, cuts, -0.22, 0.18)
    return jnp.clip(with_spikes(drawn, jax.random.fold_in(own_key, 3), *heavy), -most, most).astype(held_as)


def setup_inputs(seed: int = 0) -> dict:
    arg_keys = jax.random.split(jax.random.key(seed), 9)
    tokens = bell_draw(arg_keys[0], (TOKENS, D), 1.0, 6.0, ((0, 1024),))
    norm_gain = jnp.clip(1.0 + 0.15 * jax.random.normal(arg_keys[1], (D,), jnp.float32), 0.25, 1.75)
    router_w = bell_draw(arg_keys[2], (D, EXPERTS), D ** -0.5, 0.1875)
    w_gate = bell_draw(arg_keys[3], (EXPERTS, D, FF), D ** -0.5, 0.1875, ((0, 16),))
    w_up = bell_draw(arg_keys[4], (EXPERTS, D, FF), D ** -0.5, 0.1875, ((0, 16),))
    w_down = bell_draw(arg_keys[5], (EXPERTS, FF, D), FF ** -0.5, 0.3125, ((0, 16),))
    routes_keys = jax.random.split(jax.random.fold_in(arg_keys[6], 1), TOKENS // TOK_DEV)
    routes_turns = jax.random.permutation(jax.random.fold_in(arg_keys[6], 3), TOKENS // TOK_DEV)
    routes = jax.vmap(lambda own, number: shared_out(jax.random.fold_in(arg_keys[6], 2), own, number, TOK_DEV, EXPERTS, TOP, MOST, 2))(routes_keys, routes_turns).reshape((TOKENS, TOP))
    grad_out = bell_draw_with(arg_keys[7], (TOKENS, D), 1.0, 24.0, ((0, 1024),), (0, 1, 1024, 6.0))
    return {"tokens": tokens, "norm_gain": norm_gain, "router_w": router_w, "w_gate": w_gate, "w_up": w_up, "w_down": w_down, "routes": routes, "grad_out": grad_out}


def slot_of(routes_dev):
    flat_routes = routes_dev.reshape(-1)
    onehot = (flat_routes[:, None] == jnp.arange(EXPERTS, dtype=jnp.int32)[None, :]).astype(jnp.int32)
    before = jnp.cumsum(onehot, axis=0) - onehot
    return lax.optimization_barrier(jnp.sum(before * onehot, axis=1)).astype(jnp.int32)

def reference(tokens, norm_gain, router_w, w_gate, w_up, w_down, routes, grad_out):
    tokens_wide = tokens.astype(jnp.float32)
    inverse = lax.rsqrt(lax.optimization_barrier(jnp.mean(tokens_wide * tokens_wide, axis=1, keepdims=True)) + 1e-06)
    unit_rows = tokens_wide * inverse
    normed = (unit_rows * norm_gain).astype(jnp.bfloat16)
    logits = jnp.dot(normed, router_w, preferred_element_type=jnp.float32)
    picked = jnp.take_along_axis(logits, routes, axis=1)
    gate_pair = jnp.stack([jax.nn.sigmoid(picked[:, 0] - picked[:, 1]), jax.nn.sigmoid(picked[:, 1] - picked[:, 0])], axis=1)
    gate_wide = w_gate.astype(jnp.float32)
    up_wide = w_up.astype(jnp.float32)
    down_wide = w_down.astype(jnp.float32)
    group_rows = N_EXPERT * TOK_DEV
    buffer_rows = EXPERTS * N_EXPERT * MOST

    def group_step(totals, pieces):
        gate_total, up_total, down_total = totals
        normed_g, routes_g, gates_g, grad_g = pieces
        slot_index = jax.vmap(slot_of)(routes_g.reshape(N_EXPERT, TOK_DEV, TOP))
        source = jnp.arange(N_EXPERT, dtype=jnp.int32)[:, None]
        placement = ((routes_g.reshape(N_EXPERT, TOK_DEV * TOP) * N_EXPERT + source) * MOST + slot_index).reshape(-1)
        copied = jnp.repeat(normed_g, TOP, axis=0)
        arrived = jnp.zeros((buffer_rows, D), jnp.bfloat16).at[placement].set(copied)
        arrived_wide = arrived.reshape(EXPERTS, N_EXPERT * MOST, D).astype(jnp.float32)
        pre_gate = jnp.einsum('erd,edf->erf', arrived_wide, gate_wide)
        pre_up = jnp.einsum('erd,edf->erf', arrived_wide, up_wide)
        sigmoid_gate = jax.nn.sigmoid(pre_gate)
        active = pre_gate * sigmoid_gate
        hidden = (active * pre_up).astype(jnp.bfloat16)
        hidden_wide = hidden.astype(jnp.float32)
        produced = jnp.einsum('erf,efd->erd', hidden_wide, down_wide).astype(jnp.bfloat16)
        picked_rows = produced.reshape(buffer_rows, D)[placement].reshape(group_rows, TOP, D).astype(jnp.float32)
        layer_g = lax.optimization_barrier(jnp.sum(gates_g[:, :, None] * picked_rows, axis=1)).astype(jnp.bfloat16)
        upstream = grad_g.astype(jnp.float32)
        d_pair = lax.optimization_barrier(jnp.sum(upstream[:, None, :] * picked_rows, axis=2))
        d_rows = (gates_g[:, :, None] * upstream[:, None, :]).astype(jnp.bfloat16).reshape(-1, D)
        d_arrived = jnp.zeros((buffer_rows, D), jnp.bfloat16).at[placement].set(d_rows)
        d_arrived_wide = d_arrived.reshape(EXPERTS, N_EXPERT * MOST, D).astype(jnp.float32)
        d_hidden = jnp.einsum('erd,efd->erf', d_arrived_wide, down_wide)
        d_pre_gate = (d_hidden * pre_up * sigmoid_gate * (1.0 + pre_gate * (1.0 - sigmoid_gate))).astype(jnp.bfloat16)
        d_pre_up = (d_hidden * active).astype(jnp.bfloat16)
        d_gate_wide = d_pre_gate.astype(jnp.float32)
        d_up_wide = d_pre_up.astype(jnp.float32)
        d_back = (jnp.einsum('erf,edf->erd', d_gate_wide, gate_wide) + jnp.einsum('erf,edf->erd', d_up_wide, up_wide)).astype(jnp.bfloat16)
        d_picked = d_back.reshape(buffer_rows, D)[placement].reshape(group_rows, TOP, D).astype(jnp.float32)
        d_normed_g = lax.optimization_barrier(jnp.sum(d_picked, axis=1))
        gate_total = gate_total + jnp.einsum('erd,erf->edf', arrived_wide, d_gate_wide)
        up_total = up_total + jnp.einsum('erd,erf->edf', arrived_wide, d_up_wide)
        down_total = down_total + jnp.einsum('erf,erd->efd', hidden_wide, d_arrived_wide)
        return ((gate_total, up_total, down_total), (layer_g, d_normed_g, d_pair))
    start_totals = (jnp.zeros((EXPERTS, D, FF), jnp.float32), jnp.zeros((EXPERTS, D, FF), jnp.float32), jnp.zeros((EXPERTS, FF, D), jnp.float32))
    pieces = (normed.reshape(N_DP, group_rows, D), routes.reshape(N_DP, group_rows, TOP), gate_pair.reshape(N_DP, group_rows, TOP), grad_out.reshape(N_DP, group_rows, D))
    totals, results = lax.scan(group_step, start_totals, pieces)
    d_gate_w, d_up_w, d_down_w = totals
    layer_out = results[0].reshape(-1, D)
    d_normed = results[1].reshape(-1, D)
    d_pair = results[2].reshape(-1, TOP)
    d_first = gate_pair[:, 0] * gate_pair[:, 1] * (d_pair[:, 0] - d_pair[:, 1])
    expert_ids = jnp.arange(EXPERTS, dtype=jnp.int32)[None, :]
    d_logits = ((routes[:, 0:1] == expert_ids).astype(jnp.float32) - (routes[:, 1:2] == expert_ids).astype(jnp.float32)) * d_first[:, None]
    router_wide = router_w.astype(jnp.float32)
    d_normed = d_normed + jnp.dot(d_logits, router_wide.T, precision=lax.Precision.HIGHEST)
    d_router = jnp.dot(normed.astype(jnp.float32).T, d_logits, precision=lax.Precision.HIGHEST)
    d_gain = lax.optimization_barrier(jnp.sum(d_normed * unit_rows, axis=0))
    scaled_grad = d_normed * norm_gain
    d_tokens = (inverse * (scaled_grad - unit_rows * lax.optimization_barrier(jnp.mean(scaled_grad * unit_rows, axis=1, keepdims=True)))).astype(jnp.bfloat16)
    return (layer_out, d_tokens, d_gain, d_router, d_gate_w, d_up_w, d_down_w)
```

```python
import jax
import jax.numpy as jnp
from jax import lax
from jax.experimental import pallas as pl
from jax.experimental.pallas import tpu as pltpu
from jax.sharding import PartitionSpec as P

TOP = 2
MESH = pl.DeviceIdType.MESH
ANY = pl.BlockSpec(memory_space=pl.ANY)
VMEM = pl.BlockSpec(memory_space=pltpu.VMEM)
LIMIT = 48 * 1024 * 1024

contract_rows = (((0,), (0,)), ((), ()))
contract_cols = (((1,), (1,)), ((), ()))


class Place:
    def __init__(self):
        dp, ex = lax.axis_index("dp"), lax.axis_index("expert")
        self.y, self.zl = lax.rem(dp, 4), lax.div(dp, 4)
        self.a, self.b = lax.div(self.zl, 4), lax.rem(self.zl, 4)
        self.x, self.zh, self.core = lax.div(ex, 4), lax.rem(lax.div(ex, 2), 2), lax.rem(ex, 2)
        self.yhi = lax.div(self.y, 2)
        self.ylow = self.y + self.yhi * (3 - 2 * self.y)
        zexp = self.zh + self.yhi - 2 * self.zh * self.yhi
        self.me = self.x * 4 + zexp * 2 + self.core

    def at(self, x=None, y=None, zl=None, zh=None, core=None):
        x = self.x if x is None else x
        y = self.y if y is None else y
        zl = self.zl if zl is None else zl
        zh = self.zh if zh is None else zh
        core = self.core if core is None else core
        return (zl * 4 + y, x * 4 + zh * 2 + core)

    def member(self, h):
        x, zexp, core = lax.div(h, 4), lax.rem(lax.div(h, 2), 2), lax.rem(h, 2)
        hi = zexp + self.zh - 2 * zexp * self.zh
        return self.at(x=x, y=self.ylow + hi * (3 - 2 * self.ylow), core=core)

    def zglobal(self, step):
        z = lax.rem(self.zh * 16 + self.zl + 32 + step, 32)
        return self.at(zl=lax.rem(z, 16), zh=lax.div(z, 16))


def signal(device):
    pl.semaphore_signal(pltpu.get_barrier_semaphore(), inc=1, device_id=device, device_id_type=MESH)


def remote(src, dst, send_sem, recv_sem, device):
    return pltpu.make_async_remote_copy(
        src_ref=src, dst_ref=dst, send_sem=send_sem, recv_sem=recv_sem, device_id=device, device_id_type=MESH
    )


def exchange(place, send, recv, send_sem, recv_sem, own_sem):
    own = pltpu.make_async_copy(send.at[place.me], recv.at[place.me], own_sem)
    own.start()
    copies = []
    for k in range(1, 16):
        h = lax.rem(place.me + k, 16)
        copy = remote(send.at[h], recv.at[place.me], send_sem.at[k], recv_sem.at[k], place.member(h))
        copy.start()
        copies.append(copy)
    return own, copies


def dispatch_kernel(
    send, gate, up, down, recv, gate_out, up_out, down_out,
    send_sem, recv_sem, own_sem, first_sem, fwd_sem, side_sem, from_z, from_y, keep_sem,
):
    p = Place()
    for k in range(1, 16):
        signal(p.member(lax.rem(p.me + k, 16)))
    foreign = p.yhi == 1
    after = jnp.where(p.zl == 7, 0, 1)
    before = jnp.where(p.zl == 8, 0, 1)
    sibling = p.at(y=p.y + 1 - 2 * lax.rem(p.y, 2))

    @pl.when(foreign)
    def _():
        signal(sibling)

    @pl.when(jnp.logical_and(foreign, p.zl != 7))
    def _():
        signal(p.zglobal(1))

    @pl.when(jnp.logical_and(foreign, p.zl != 8))
    def _():
        signal(p.zglobal(-1))

    pl.semaphore_wait(pltpu.get_barrier_semaphore(), 15 + p.yhi * (1 + after + before))

    pairs = ((gate, gate_out), (up, up_out), (down, down_out))
    rows = [src.shape[0] // 8 for src, _ in pairs]
    half = lax.rem(p.y, 2)

    def piece(n, ref, side, c):
        return ref.at[pl.ds(pl.multiple_of((side * 4 + c) * rows[n], 16), rows[n])]

    def boundary(n, c, to):
        src, dst = pairs[n]
        return remote(
            piece(n, src, half, c), piece(n, dst, half, c), first_sem.at[n * 4 + c], from_z.at[n * 4 + c], to
        )

    def onward(n, c, to):
        dst = pairs[n][1]
        return remote(piece(n, dst, half, c), piece(n, dst, half, c), fwd_sem.at[n * 4 + c], from_z.at[n * 4 + c], to)

    def sideways(n, c):
        dst = pairs[n][1]
        return remote(
            piece(n, dst, half, c), piece(n, dst, half, c), side_sem.at[n * 4 + c], from_y.at[n * 4 + c], sibling
        )

    def each(body):
        for n in range(3):
            def step(c, carry, n=n):
                body(n, c)
                return carry
            lax.fori_loop(0, 4, step, 0)

    edge = jnp.logical_or(p.zl == 0, p.zl == 15)
    outward = p.zglobal(jnp.where(p.zl == 0, -1, 1))
    inward = p.at(zl=p.zl + jnp.where(p.zl < 8, 1, -1))
    passes = jnp.logical_and(p.zl != 7, p.zl != 8)

    @pl.when(jnp.logical_and(foreign, edge))
    def _():
        each(lambda n, c: boundary(n, c, outward).start())

    own, copies = exchange(p, send, recv, send_sem, recv_sem, own_sem)

    @pl.when(jnp.logical_not(foreign))
    def _():
        kept = [pltpu.make_async_copy(src, dst, keep_sem.at[n]) for n, (src, dst) in enumerate(pairs)]
        for copy in kept:
            copy.start()
        for copy in kept:
            copy.wait()

    @pl.when(foreign)
    def _():
        def take(n, c):
            onward(n, c, inward).wait_recv()

            @pl.when(passes)
            def _():
                onward(n, c, inward).start()

            sideways(n, c).start()

        each(take)
        each(lambda n, c: sideways(n, c).wait())

    @pl.when(jnp.logical_and(foreign, passes))
    def _():
        each(lambda n, c: onward(n, c, inward).wait_send())

    @pl.when(jnp.logical_and(foreign, edge))
    def _():
        each(lambda n, c: boundary(n, c, outward).wait_send())

    own.wait()
    for copy in copies:
        copy.wait()


def dispatch(send, gate, up, down):
    dma = pltpu.SemaphoreType.DMA
    return pl.pallas_call(
        dispatch_kernel,
        out_shape=[jax.ShapeDtypeStruct(v.shape, v.dtype) for v in (send, gate, up, down)],
        in_specs=[ANY] * 4,
        out_specs=[ANY] * 4,
        scratch_shapes=[
            dma((16,)), dma((16,)), dma(()), dma((12,)), dma((12,)), dma((12,)), dma((12,)), dma((12,)), dma((3,)),
        ],
        compiler_params=pltpu.CompilerParams(collective_id=0, has_side_effects=True, vmem_limit_bytes=LIMIT),
    )(send, gate, up, down)


def return_kernel(
    send, part, recv, total,
    y_got, held, z_got, send_sem, recv_sem, own_sem, y_send, y_recv, z_send, z_recv,
):
    p = Place()
    sibling = p.at(y=p.y + 1 - 2 * lax.rem(p.y, 2))
    for k in range(1, 16):
        signal(p.member(lax.rem(p.me + k, 16)))
    signal(sibling)
    for k in range(1, 4):
        signal(p.at(zl=p.a * 4 + lax.rem(p.b + k, 4)))
    pl.semaphore_wait(pltpu.get_barrier_semaphore(), 19)

    side = p.ylow
    y_copies = []
    for k in range(4):
        bb = lax.rem(p.b + k + 1, 4)
        copy = remote(part.at[1 - side, bb], y_got.at[bb], y_send.at[k], y_recv.at[k], sibling)
        copy.start()
        y_copies.append(copy)
    own, copies = exchange(p, send, recv, send_sem, recv_sem, own_sem)
    z_copies = []
    for k in range(4):
        bb = lax.rem(p.b + k + 1, 4)
        y_copies[k].wait_recv()
        both = part[side, bb].astype(jnp.float32) + y_got[bb].astype(jnp.float32)
        if k == 3:
            for copy in z_copies:
                copy.wait_recv()
            for j in range(3):
                both = both + z_got[j].astype(jnp.float32)
            total[...] = both.astype(jnp.bfloat16)
        else:
            held[k] = both.astype(jnp.bfloat16)
            copy = remote(held.at[k], z_got.at[k], z_send.at[k], z_recv.at[k], p.at(zl=p.a * 4 + bb))
            copy.start()
            z_copies.append(copy)
    for copy in y_copies + z_copies:
        copy.wait_send()
    own.wait()
    for copy in copies:
        copy.wait()


def give_back(send, part):
    dma = pltpu.SemaphoreType.DMA
    block = part.shape[2:]
    return pl.pallas_call(
        return_kernel,
        out_shape=[jax.ShapeDtypeStruct(send.shape, send.dtype), jax.ShapeDtypeStruct(block, jnp.bfloat16)],
        in_specs=[ANY, VMEM],
        out_specs=[ANY, VMEM],
        scratch_shapes=[
            pltpu.VMEM((4,) + block, jnp.bfloat16),
            pltpu.VMEM((3,) + block, jnp.bfloat16),
            pltpu.VMEM((3,) + block, jnp.bfloat16),
            dma((16,)), dma((16,)), dma(()), dma((4,)), dma((4,)), dma((3,)), dma((3,)),
        ],
        compiler_params=pltpu.CompilerParams(collective_id=1, has_side_effects=True, vmem_limit_bytes=LIMIT),
    )(send, part)


def finish_kernel(
    part, small, share, small_out,
    z_got, leaving, native, other, g1, mine, g2, g3, g4, whole,
    z_send, z_recv, f_send, f_recv, s1, r1, s2, r2, s3, r3, s4, r4, s5, r5,
):
    p = Place()
    xc = p.x * 2 + p.core

    def xc_at(t):
        return p.at(x=lax.div(t, 2), core=lax.rem(t, 2))

    def y_at(t):
        return p.at(y=t)

    def b_at(t):
        return p.at(zl=p.a * 4 + t)

    def c_at(t):
        return p.at(zl=lax.rem(t, 4) * 4 + p.b, zh=lax.div(t, 4))

    ci = p.zh * 4 + p.a
    for k in range(1, 8):
        signal(xc_at(lax.rem(xc + k, 8)))
        signal(c_at(lax.rem(ci + k, 8)))
    for k in range(1, 4):
        signal(y_at(lax.rem(p.y + k, 4)))
        signal(b_at(lax.rem(p.b + k, 4)))
    signal(p.at(y=3 - p.y, zh=1 - p.zh))
    pl.semaphore_wait(pltpu.get_barrier_semaphore(), 21)

    z_copies = []
    for k in range(3):
        aa = lax.rem(p.a + k + 1, 4)
        copy = remote(part.at[aa], z_got.at[k], z_send.at[k], z_recv.at[k], p.at(zl=aa * 4 + p.b))
        copy.start()
        z_copies.append(copy)

    def lanes(t):
        return pl.ds(pl.multiple_of(t * 128, 128), 128)

    first = []
    for k in range(1, 8):
        t = lax.rem(xc + k, 8)
        copy = remote(small.at[:, lanes(t)], g1.at[k], s1.at[k], r1.at[k], xc_at(t))
        copy.start()
        first.append(copy)

    value = small[:, lanes(xc)]
    for copy in first:
        copy.wait()
    for k in range(1, 8):
        value = value + g1[k]

    def everywhere(value, slots, n, index, where, send_sem, recv_sem, stage):
        slots[index] = value
        copies = []
        for k in range(1, n):
            copy = remote(
                slots.at[index], slots.at[index], send_sem.at[k], recv_sem.at[k], where(lax.rem(index + k, n))
            )
            copy.start()
            copies.append(copy)
        for copy in copies:
            copy.wait()
        value = slots[0]
        for k in range(1, n):
            value = value + slots[k]
        return value

    value = everywhere(value, g2, 4, p.y, y_at, s2, r2, 0)
    value = everywhere(value, g3, 4, p.b, b_at, s3, r3, 1)

    for copy in z_copies:
        copy.wait()
    summed = part[p.a].astype(jnp.float32)
    for k in range(3):
        summed = summed + z_got[k].astype(jnp.float32)
    leaving[...] = summed.astype(jnp.bfloat16).reshape(leaving.shape)
    native_rows = summed[: summed.shape[0] // 2]

    foreign = p.yhi == 1
    to_native = remote(leaving.at[1], native, f_send.at[0], f_recv.at[0], p.at(y=3 - p.y))
    cross_low = remote(leaving.at[0], other, f_send.at[0], f_recv.at[1], p.at(y=3 - p.y, zh=1 - p.zh))
    cross_high = remote(leaving.at[1], other, f_send.at[1], f_recv.at[1], p.at(zh=1 - p.zh))

    @pl.when(jnp.logical_not(foreign))
    def _():
        to_native.start()

    @pl.when(foreign)
    def _():
        cross_low.start()
        cross_high.start()

    value = everywhere(value, g4, 8, ci, c_at, s4, r4, 2)
    whole[...] = value
    small_out[:, lanes(xc)] = value
    last = []
    for k in range(1, 8):
        copy = remote(whole, small_out.at[:, lanes(xc)], s5.at[k], r5.at[k], xc_at(lax.rem(xc + k, 8)))
        copy.start()
        last.append(copy)

    cross_high.wait_recv()

    @pl.when(jnp.logical_not(foreign))
    def _():
        to_native.wait_send()
        share[...] = native_rows + other[...].astype(jnp.float32)

    @pl.when(foreign)
    def _():
        cross_low.wait_send()
        cross_high.wait_send()
        to_native.wait_recv()
        share[...] = native[...].astype(jnp.float32) + other[...].astype(jnp.float32)

    for copy in last:
        copy.wait()


def finish(part, small):
    dma = pltpu.SemaphoreType.DMA
    rows, width = part.shape[1] // 2, part.shape[2]
    tall = small.shape[0]
    f32 = jnp.float32
    return pl.pallas_call(
        finish_kernel,
        out_shape=[jax.ShapeDtypeStruct((rows, width), f32), jax.ShapeDtypeStruct(small.shape, f32)],
        in_specs=[VMEM, VMEM],
        out_specs=[VMEM, VMEM],
        scratch_shapes=[
            pltpu.VMEM((3, 2 * rows, width), jnp.bfloat16),
            pltpu.VMEM((2, rows, width), jnp.bfloat16),
            pltpu.VMEM((rows, width), jnp.bfloat16),
            pltpu.VMEM((rows, width), jnp.bfloat16),
            pltpu.VMEM((8, tall, 128), f32),
            pltpu.VMEM((tall, 128), f32),
            pltpu.VMEM((4, tall, 128), f32),
            pltpu.VMEM((4, tall, 128), f32),
            pltpu.VMEM((8, tall, 128), f32),
            pltpu.VMEM((tall, 128), f32),
            dma((3,)), dma((3,)), dma((2,)), dma((2,)),
            dma((8,)), dma((8,)), dma((4,)), dma((4,)), dma((4,)), dma((4,)),
            dma((8,)), dma((8,)), dma((8,)), dma((8,)),
        ],
        compiler_params=pltpu.CompilerParams(collective_id=2, has_side_effects=True, vmem_limit_bytes=LIMIT),
    )(part, small)


def local(tokens, norm_gain, router_w, w_gate, w_up, w_down, routes, grad_out):
    f32, bf16 = jnp.float32, jnp.bfloat16
    tok_dev, width = tokens.shape
    experts = lax.axis_size("expert")
    capacity = max(2, 3 * tok_dev * TOP // (2 * experts))
    tokens_wide = tokens.astype(f32)
    inverse = lax.rsqrt(jnp.mean(tokens_wide * tokens_wide, axis=1, keepdims=True) + 1e-06)
    unit_rows = tokens_wide * inverse
    normed = (unit_rows * norm_gain).astype(bf16)
    logits = jnp.dot(normed, router_w, preferred_element_type=f32)
    expert_ids = jnp.arange(experts, dtype=jnp.int32)[None, :]
    chosen = [routes[:, k : k + 1] == expert_ids for k in range(TOP)]
    picked = [jnp.sum(jnp.where(hot, logits, 0.0), axis=1) for hot in chosen]
    gate_pair = [jax.nn.sigmoid(picked[0] - picked[1]), jax.nn.sigmoid(picked[1] - picked[0])]

    token_ids = jnp.arange(tok_dev, dtype=jnp.int32)
    earlier = (token_ids[:, None] > token_ids[None, :]).astype(bf16)
    named = jnp.logical_or(chosen[0], chosen[1]).astype(bf16)
    ahead = jnp.dot(earlier, named, preferred_element_type=f32)
    slots = [
        routes[:, k] * (2 * capacity) + jnp.sum(jnp.where(chosen[k], ahead, 0.0), axis=1).astype(jnp.int32)
        for k in range(TOP)
    ]
    places = jnp.arange(experts * 2 * capacity, dtype=jnp.int32)
    hits = [places[:, None] == slot[None, :] for slot in slots]
    d_hits = [places[:, None] == slot[None, :] + capacity for slot in slots]
    pick = jnp.concatenate(
        [jnp.logical_or(hits[0], hits[1]).astype(bf16), jnp.logical_or(d_hits[0], d_hits[1]).astype(bf16)], axis=1
    )
    scale = jnp.sum(
        jnp.where(d_hits[0], gate_pair[0][None, :], 0.0) + jnp.where(d_hits[1], gate_pair[1][None, :], 0.0), axis=1
    )
    is_row = lax.rem(places, 2 * capacity) < capacity
    scale = jnp.where(is_row, 1.0, scale)
    stacked = jnp.concatenate([normed, grad_out], axis=0)
    send = (jnp.dot(pick, stacked, preferred_element_type=f32) * scale[:, None]).astype(bf16)
    arrived_both, gate_local, up_local, down_local = dispatch(
        send.reshape(experts, 2 * capacity, width), w_gate[0], w_up[0], w_down[0]
    )
    arrived = arrived_both[:, :capacity].reshape(-1, width)
    d_arrived = arrived_both[:, capacity:].reshape(-1, width)

    pre_gate = jnp.dot(arrived, gate_local, preferred_element_type=f32)
    pre_up = jnp.dot(arrived, up_local, preferred_element_type=f32)
    sigmoid_gate = jax.nn.sigmoid(pre_gate)
    active = pre_gate * sigmoid_gate
    hidden = (active * pre_up).astype(bf16)
    produced = jnp.dot(hidden, down_local, preferred_element_type=f32).astype(bf16)
    d_hidden = lax.dot_general(d_arrived, down_local, contract_cols, preferred_element_type=f32)
    d_pre_gate = (d_hidden * pre_up * sigmoid_gate * (1.0 + pre_gate * (1.0 - sigmoid_gate))).astype(bf16)
    d_pre_up = (d_hidden * active).astype(bf16)
    d_back = (
        lax.dot_general(d_pre_gate, gate_local, contract_cols, preferred_element_type=f32)
        + lax.dot_general(d_pre_up, up_local, contract_cols, preferred_element_type=f32)
    ).astype(bf16)
    hidden_units = gate_local.shape[1]
    d_pre_both = jnp.concatenate([d_pre_gate, d_pre_up], axis=1)
    joined = jnp.concatenate(
        [
            lax.dot_general(arrived, d_pre_both, contract_rows, preferred_element_type=f32).astype(bf16),
            lax.dot_general(d_arrived, hidden, contract_rows, preferred_element_type=f32).astype(bf16),
        ],
        axis=1,
    )
    rows = width // lax.axis_size("dp")
    blocks = joined.reshape(4, 4, 4, rows, 3 * hidden_units)
    halves = [jnp.stack([blocks[:, :, i], blocks[:, :, 3 - i]], axis=2) for i in range(2)]
    part = jnp.stack(halves, axis=0).transpose(0, 2, 1, 3, 4, 5).reshape(2, 4, 8 * rows, 3 * hidden_units)

    back = jnp.concatenate(
        [produced.reshape(experts, capacity, width), d_back.reshape(experts, capacity, width)], axis=1
    )
    returned, part = give_back(back, part)
    returned = returned.reshape(-1, width)
    pull = jnp.concatenate([hits[0], hits[1], jnp.logical_or(d_hits[0], d_hits[1])], axis=1).astype(bf16)
    pulled = lax.dot_general(pull, returned, contract_rows, preferred_element_type=f32)
    rows_0, rows_1, d_normed = pulled[:tok_dev], pulled[tok_dev : 2 * tok_dev], pulled[2 * tok_dev :]
    layer_out = (gate_pair[0][:, None] * rows_0 + gate_pair[1][:, None] * rows_1).astype(bf16)
    upstream = grad_out.astype(f32)
    d_pair = [jnp.sum(upstream * rows_0, axis=1), jnp.sum(upstream * rows_1, axis=1)]
    d_first = gate_pair[0] * gate_pair[1] * (d_pair[0] - d_pair[1])
    d_logits = (chosen[0].astype(f32) - chosen[1].astype(f32)) * d_first[:, None]
    router_wide = router_w.astype(f32)
    d_normed = d_normed + lax.dot_general(d_logits, router_wide, contract_cols, precision=lax.Precision.HIGHEST)
    router_term = lax.dot_general(d_logits, normed.astype(f32), contract_rows, precision=lax.Precision.HIGHEST)
    gain_term = jnp.sum(d_normed * unit_rows, axis=0, keepdims=True)
    small = jnp.concatenate([router_term, gain_term, jnp.zeros((24 - experts - 1, width), f32)], axis=0)
    share, small = finish(part.reshape(4, 2 * rows, 3 * hidden_units), small)
    scaled_grad = d_normed * norm_gain
    d_tokens = (
        inverse * (scaled_grad - unit_rows * jnp.mean(scaled_grad * unit_rows, axis=1, keepdims=True))
    ).astype(bf16)
    return (
        layer_out,
        d_tokens,
        small[experts],
        jnp.transpose(small[:experts]),
        share[None, :, :hidden_units],
        share[None, :, hidden_units : 2 * hidden_units],
        jnp.transpose(share[:, 2 * hidden_units :])[None],
    )


def solution(mesh):
    rows, experts, copied = P(("dp", "expert"), None), P("expert", None, None), P()
    return jax.shard_map(
        local,
        mesh=mesh,
        in_specs=(rows, copied, copied, experts, experts, experts, rows, rows),
        out_specs=(
            rows,
            rows,
            copied,
            copied,
            P("expert", "dp", None),
            P("expert", "dp", None),
            P("expert", None, "dp"),
        ),
        check_vma=False,
    )
```

```python
import jax
import jax.numpy as jnp
from jax import lax
from jax.experimental import pallas as pl
from jax.experimental.pallas import tpu as pltpu
from jax.sharding import PartitionSpec as P

TOP = 2
MESH = pl.DeviceIdType.MESH
ANY = pl.BlockSpec(memory_space=pl.ANY)
VMEM = pl.BlockSpec(memory_space=pltpu.VMEM)
LIMIT = 48 * 1024 * 1024

contract_rows = (((0,), (0,)), ((), ()))
contract_cols = (((1,), (1,)), ((), ()))


class Place:
    def __init__(self):
        dp, ex = lax.axis_index("dp"), lax.axis_index("expert")
        self.y, self.zl = lax.rem(dp, 4), lax.div(dp, 4)
        self.a, self.b = lax.div(self.zl, 4), lax.rem(self.zl, 4)
        self.x, self.zh, self.core = lax.div(ex, 4), lax.rem(lax.div(ex, 2), 2), lax.rem(ex, 2)
        self.far = lax.rem(lax.div(self.y + 1, 2) + 1, 2)
        self.side = lax.div(self.y, 2)
        self.zexp = self.zh + self.far - 2 * self.zh * self.far
        self.me = self.x * 4 + self.zexp * 2 + self.core

    def at(self, x=None, y=None, zl=None, zh=None, core=None):
        x = self.x if x is None else x
        y = self.y if y is None else y
        zl = self.zl if zl is None else zl
        zh = self.zh if zh is None else zh
        core = self.core if core is None else core
        return (zl * 4 + y, x * 4 + zh * 2 + core)

    def worker(self, far):
        return (1 - far) * (1 - self.side) + (2 + far) * self.side

    def member(self, h):
        x, zexp, core = lax.div(h, 4), lax.rem(lax.div(h, 2), 2), lax.rem(h, 2)
        return self.at(x=x, y=self.worker(zexp + self.zh - 2 * zexp * self.zh), core=core)

    def zglobal(self, step):
        z = lax.rem(self.zh * 16 + self.zl + 32 + step, 32)
        return self.at(zl=lax.rem(z, 16), zh=lax.div(z, 16))


def signal(device):
    pl.semaphore_signal(pltpu.get_barrier_semaphore(), inc=1, device_id=device, device_id_type=MESH)


def remote(src, dst, send_sem, recv_sem, device):
    return pltpu.make_async_remote_copy(
        src_ref=src, dst_ref=dst, send_sem=send_sem, recv_sem=recv_sem, device_id=device, device_id_type=MESH
    )


def exchange(place, send, recv, send_sem, recv_sem, own_sem):
    own = pltpu.make_async_copy(send.at[place.me], recv.at[place.me], own_sem)
    own.start()
    copies = []
    for k in range(1, 16):
        h = lax.rem(place.me + k, 16)
        copy = remote(send.at[h], recv.at[place.me], send_sem.at[k], recv_sem.at[k], place.member(h))
        copy.start()
        copies.append(copy)
    return own, copies


def dispatch_kernel(
    send, gate, up, down, recv, gate_out, up_out, down_out,
    send_sem, recv_sem, own_sem, first_sem, fwd_sem, side_sem, from_z, from_y, keep_sem,
):
    p = Place()
    for k in range(1, 16):
        signal(p.member(lax.rem(p.me + k, 16)))
    far = p.far == 1
    after = jnp.where(p.zl == 7, 0, 1)
    before = jnp.where(p.zl == 8, 0, 1)
    sibling = p.at(y=3 - p.y)

    @pl.when(far)
    def _():
        signal(sibling)

    @pl.when(jnp.logical_and(far, p.zl != 7))
    def _():
        signal(p.zglobal(1))

    @pl.when(jnp.logical_and(far, p.zl != 8))
    def _():
        signal(p.zglobal(-1))

    pl.semaphore_wait(pltpu.get_barrier_semaphore(), 15 + p.far * (1 + after + before))

    pairs = ((gate, gate_out, 8), (up, up_out, 8), (down, down_out, 6))
    first_of = (0, 8, 16)

    def piece(n, ref, c):
        half = pairs[n][0].shape[0] // 2
        step = half // pairs[n][2]
        return ref.at[pl.ds(pl.multiple_of(p.side * half + c * step, 16), step)]

    def boundary(n, c, to):
        i = first_of[n] + c
        return remote(piece(n, pairs[n][0], c), piece(n, pairs[n][1], c), first_sem.at[i], from_z.at[i], to)

    def onward(n, c, to):
        i = first_of[n] + c
        return remote(piece(n, pairs[n][1], c), piece(n, pairs[n][1], c), fwd_sem.at[i], from_z.at[i], to)

    def sideways(n, c):
        i = first_of[n] + c
        return remote(piece(n, pairs[n][1], c), piece(n, pairs[n][1], c), side_sem.at[i], from_y.at[i], sibling)

    def each(body):
        for n in range(3):
            def step(c, carry, n=n):
                body(n, c)
                return carry
            lax.fori_loop(0, pairs[n][2], step, 0)

    edge = jnp.logical_and(far, jnp.logical_or(p.zl == 0, p.zl == 15))
    outward = p.zglobal(jnp.where(p.zl == 0, -1, 1))
    inward = p.at(zl=p.zl + jnp.where(p.zl < 8, 1, -1))
    passes = jnp.logical_and(far, jnp.logical_and(p.zl != 7, p.zl != 8))

    @pl.when(edge)
    def _():
        each(lambda n, c: boundary(n, c, outward).start())

    own = pltpu.make_async_copy(send.at[p.me], recv.at[p.me], own_sem)
    own.start()

    def rows_to(k):
        h = lax.rem(p.me + k, 16)
        return remote(send.at[h], recv.at[p.me], send_sem.at[k], recv_sem.at[k], p.member(h))

    def every(first, body):
        def step(k, carry):
            body(k)
            return carry
        lax.fori_loop(first, 16, step, 0)

    @pl.when(jnp.logical_not(far))
    def _():
        every(1, lambda k: rows_to(k).start())
        kept = [pltpu.make_async_copy(pairs[n][0], pairs[n][1], keep_sem.at[n]) for n in range(3)]
        for copy in kept:
            copy.start()
        for copy in kept:
            copy.wait()

    @pl.when(far)
    def _():
        def take(n, c):
            onward(n, c, inward).wait_recv()

            @pl.when(passes)
            def _():
                onward(n, c, inward).start()

            sideways(n, c).start()

            @pl.when(first_of[n] + c < 15)
            def _():
                rows_to(first_of[n] + c + 1).start()

        each(take)
        each(lambda n, c: sideways(n, c).wait())

    @pl.when(passes)
    def _():
        each(lambda n, c: onward(n, c, inward).wait_send())

    @pl.when(edge)
    def _():
        each(lambda n, c: boundary(n, c, outward).wait_send())

    own.wait()
    every(1, lambda k: rows_to(k).wait())


def dispatch(send, gate, up, down):
    dma = pltpu.SemaphoreType.DMA
    return pl.pallas_call(
        dispatch_kernel,
        out_shape=[jax.ShapeDtypeStruct(v.shape, v.dtype) for v in (send, gate, up, down)],
        in_specs=[ANY] * 4,
        out_specs=[ANY] * 4,
        scratch_shapes=[
            dma((16,)), dma((16,)), dma(()), dma((22,)), dma((22,)), dma((22,)), dma((22,)), dma((22,)), dma((3,)),
        ],
        compiler_params=pltpu.CompilerParams(collective_id=0, has_side_effects=True, vmem_limit_bytes=LIMIT),
    )(send, gate, up, down)


def expert_kernel(recv, gate, up, down, back, part):
    f32, bf16 = jnp.float32, jnp.bfloat16
    sources, both, width = recv.shape
    capacity, units = both // 2, gate.shape[1]
    wide = recv[...].astype(f32)
    arrived = wide[:, :capacity].reshape(-1, width).astype(bf16)
    d_arrived = wide[:, capacity:].reshape(-1, width).astype(bf16)
    pre_gate = jnp.dot(arrived, gate[...], preferred_element_type=f32)
    pre_up = jnp.dot(arrived, up[...], preferred_element_type=f32)
    d_hidden = lax.dot_general(d_arrived, down[...], contract_cols, preferred_element_type=f32)
    sigmoid_gate = jax.nn.sigmoid(pre_gate)
    active = pre_gate * sigmoid_gate
    hidden = (active * pre_up).astype(bf16)
    d_pre_gate = (d_hidden * pre_up * sigmoid_gate * (1.0 + pre_gate * (1.0 - sigmoid_gate))).astype(bf16)
    d_pre_up = (d_hidden * active).astype(bf16)
    produced = jnp.dot(hidden, down[...], preferred_element_type=f32)
    d_back = lax.dot_general(
        d_pre_gate, gate[...], contract_cols, preferred_element_type=f32
    ) + lax.dot_general(d_pre_up, up[...], contract_cols, preferred_element_type=f32)
    back[...] = jnp.concatenate(
        [produced.reshape(sources, capacity, width), d_back.reshape(sources, capacity, width)], axis=1
    ).astype(bf16)
    for n, (left, right) in enumerate(((arrived, d_pre_gate), (arrived, d_pre_up), (d_arrived, hidden))):
        part[:, n * units : (n + 1) * units] = lax.dot_general(
            left, right, contract_rows, preferred_element_type=f32
        ).astype(bf16)


def expert(recv, gate, up, down):
    return pl.pallas_call(
        expert_kernel,
        out_shape=[
            jax.ShapeDtypeStruct(recv.shape, recv.dtype),
            jax.ShapeDtypeStruct((recv.shape[2], 3 * gate.shape[1]), jnp.bfloat16),
        ],
        in_specs=[VMEM] * 4,
        out_specs=[VMEM] * 2,
        compiler_params=pltpu.CompilerParams(vmem_limit_bytes=LIMIT),
    )(recv, gate, up, down)


def finish_kernel(
    send, part, pull, tokens, normed, grad, columns, signs, router, gain,
    layer_out, d_tokens, share, small_out,
    recv, y_got, held, z_got, total, got, exact, leaving, native, other, small, g1, g2, g3, g4, whole,
    send_sem, recv_sem, own_sem, y_send, y_recv, z_send, z_recv, w_send, w_recv, f_send, f_recv,
    s1, r1, s2, r2, s3, r3, s4, r4, s5, r5,
):
    f32, bf16 = jnp.float32, jnp.bfloat16
    p = Place()
    xc = p.x * 2 + p.core
    ci = p.zh * 4 + p.a

    def xc_at(t):
        return p.at(x=lax.div(t, 2), core=lax.rem(t, 2))

    def y_at(t):
        return p.at(y=t)

    def b_at(t):
        return p.at(zl=p.a * 4 + t)

    def c_at(t):
        return p.at(zl=lax.rem(t, 4) * 4 + p.b, zh=lax.div(t, 4))

    near = p.far == 0
    for k in range(1, 16):
        signal(p.member(lax.rem(p.me + k, 16)))
    for k in range(1, 8):
        signal(c_at(lax.rem(ci + k, 8)))
    for k in range(1, 4):
        signal(y_at(lax.rem(p.y + k, 4)))
        signal(b_at(lax.rem(p.b + k, 4)))
    pair = 2 * p.side + lax.rem(p.y + 1, 2)
    signal(p.at(y=pair, zh=1 - p.zh))
    pl.semaphore_wait(pltpu.get_barrier_semaphore(), 29)

    y_copies = []
    for k in range(4):
        bb = lax.rem(p.b + k + 1, 4)
        copy = remote(part.at[:, bb, 1 - p.side], y_got.at[:, bb], y_send.at[k], y_recv.at[k], p.at(y=3 - p.y))
        copy.start()
        y_copies.append(copy)
    own, copies = exchange(p, send, recv, send_sem, recv_sem, own_sem)
    z_copies = []
    for k in range(4):
        bb = lax.rem(p.b + k + 1, 4)
        y_copies[k].wait_recv()
        held[k] = (part[:, bb, p.side].astype(f32) + y_got[:, bb].astype(f32)).astype(bf16)
        if k < 3:
            copy = remote(held.at[k], z_got.at[k], z_send.at[k], z_recv.at[k], b_at(bb))
            copy.start()
            z_copies.append(copy)

    for copy in z_copies:
        copy.wait()
    summed = held[3].astype(f32)
    for k in range(3):
        summed = summed + z_got[k].astype(f32)
    total[...] = summed.astype(bf16).reshape(total.shape)

    w_copies = []
    for k in range(1, 4):
        aa = lax.rem(p.a + k, 4)
        copy = remote(total.at[aa], got.at[k - 1], w_send.at[k], w_recv.at[k], p.at(zl=aa * 4 + p.b))
        copy.start()
        w_copies.append(copy)

    own.wait()
    for copy in copies:
        copy.wait()
    returned = recv[...].reshape(-1, recv.shape[2])
    tok = tokens.shape[0]
    inverse, gate_0, gate_1 = columns[:, 0:1], columns[:, 1:2], columns[:, 2:3]
    rows_0 = jnp.dot(pull[:tok], returned, preferred_element_type=f32)
    rows_1 = jnp.dot(pull[tok : 2 * tok], returned, preferred_element_type=f32)
    layer_out[...] = (gate_0 * rows_0 + gate_1 * rows_1).astype(bf16)
    upstream = grad[...].astype(f32)
    d_pair_0 = jnp.sum(upstream * rows_0, axis=1, keepdims=True)
    d_pair_1 = jnp.sum(upstream * rows_1, axis=1, keepdims=True)
    d_logits = signs[...] * (gate_0 * gate_1 * (d_pair_0 - d_pair_1))
    high = d_logits.astype(bf16)
    rest = d_logits - high.astype(f32)
    middle = rest.astype(bf16)
    low = (rest - middle.astype(f32)).astype(bf16)
    d_normed = jnp.dot(pull[2 * tok :], returned, preferred_element_type=f32)
    for term in (low, middle, high):
        d_normed = d_normed + jnp.dot(term, router[...], preferred_element_type=f32)
    router_term = jnp.zeros((signs.shape[1], normed.shape[1]), f32)
    for term in (low, middle, high):
        router_term = router_term + lax.dot_general(term, normed[...], contract_rows, preferred_element_type=f32)
    experts = signs.shape[1]
    unit_rows = tokens[...].astype(f32) * inverse
    product = d_normed * unit_rows
    small[:experts] = router_term
    small[experts:] = jnp.broadcast_to(jnp.sum(product, axis=0, keepdims=True), (8, normed.shape[1]))
    scaled = d_normed * gain[...]
    mean = jnp.sum(product * gain[...], axis=1, keepdims=True) * (1.0 / normed.shape[1])
    d_tokens[...] = (inverse * (scaled - unit_rows * mean)).astype(bf16)

    def lanes(t):
        return pl.ds(pl.multiple_of(t * 128, 128), 128)

    first = []
    for k in range(1, 8):
        t = lax.rem(xc + k, 8)
        copy = remote(small.at[:, lanes(t)], g1.at[k], s1.at[k], r1.at[k], xc_at(t))
        copy.start()
        first.append(copy)

    value = small[:, lanes(xc)]
    for copy in first:
        copy.wait()
    for k in range(1, 8):
        value = value + g1[k]

    def everywhere(value, slots, n, index, where, send_sem, recv_sem):
        slots[index] = value
        copies = []
        for k in range(1, n):
            copy = remote(
                slots.at[index], slots.at[index], send_sem.at[k], recv_sem.at[k], where(lax.rem(index + k, n))
            )
            copy.start()
            copies.append(copy)
        for copy in copies:
            copy.wait()
        value = slots[0]
        for k in range(1, n):
            value = value + slots[k]
        return value

    value = everywhere(value, g2, 4, p.y, y_at, s2, r2)
    value = everywhere(value, g3, 4, p.b, b_at, s3, r3)

    for copy in w_copies:
        copy.wait()
    block = total[p.a].astype(f32)
    for k in range(3):
        block = block + got[k].astype(f32)
    exact[...] = block
    leaving[...] = block.astype(bf16)
    here, there = lax.rem(p.y, 2), lax.rem(p.y + 1, 2)
    to_pair = remote(leaving.at[there], native, f_send.at[0], f_recv.at[0], p.at(y=pair))
    over_same = remote(leaving.at[here], other, f_send.at[0], f_recv.at[1], p.at(zh=1 - p.zh))
    over_pair = remote(leaving.at[there], other, f_send.at[1], f_recv.at[1], p.at(y=pair, zh=1 - p.zh))

    @pl.when(near)
    def _():
        to_pair.start()

    @pl.when(jnp.logical_not(near))
    def _():
        over_same.start()
        over_pair.start()

    value = everywhere(value, g4, 8, ci, c_at, s4, r4)
    whole[...] = value
    small_out[:, lanes(xc)] = value
    last = []
    for k in range(1, 8):
        copy = remote(whole, small_out.at[:, lanes(xc)], s5.at[k], r5.at[k], xc_at(lax.rem(xc + k, 8)))
        copy.start()
        last.append(copy)

    over_same.wait_recv()

    @pl.when(near)
    def _():
        to_pair.wait_send()
        share[...] = exact[here] + other[...].astype(f32)

    @pl.when(jnp.logical_not(near))
    def _():
        over_same.wait_send()
        over_pair.wait_send()
        to_pair.wait_recv()
        share[...] = native[...].astype(f32) + other[...].astype(f32)

    for copy in y_copies:
        copy.wait_send()
    for copy in last:
        copy.wait()


def finish(send, part, pull, tokens, normed, grad, columns, signs, router, gain):
    dma = pltpu.SemaphoreType.DMA
    rows, width = part.shape[3] // 2, part.shape[4]
    features, tall = tokens.shape[1], signs.shape[1] + 8
    f32, bf16 = jnp.float32, jnp.bfloat16
    block = (4, 2 * rows, width)
    return pl.pallas_call(
        finish_kernel,
        out_shape=[
            jax.ShapeDtypeStruct(tokens.shape, bf16),
            jax.ShapeDtypeStruct(tokens.shape, bf16),
            jax.ShapeDtypeStruct((rows, width), f32),
            jax.ShapeDtypeStruct((tall, features), f32),
        ],
        in_specs=[ANY] + [VMEM] * 9,
        out_specs=[VMEM] * 4,
        scratch_shapes=[
            pltpu.VMEM(send.shape, bf16),
            pltpu.VMEM((4,) + block, bf16),
            pltpu.VMEM((4,) + block, bf16),
            pltpu.VMEM((3,) + block, bf16),
            pltpu.VMEM((4, 2, rows, width), bf16),
            pltpu.VMEM((3, 2, rows, width), bf16),
            pltpu.VMEM((2, rows, width), f32),
            pltpu.VMEM((2, rows, width), bf16),
            pltpu.VMEM((rows, width), bf16),
            pltpu.VMEM((rows, width), bf16),
            pltpu.VMEM((tall, features), f32),
            pltpu.VMEM((8, tall, 128), f32),
            pltpu.VMEM((4, tall, 128), f32),
            pltpu.VMEM((4, tall, 128), f32),
            pltpu.VMEM((8, tall, 128), f32),
            pltpu.VMEM((tall, 128), f32),
            dma((16,)), dma((16,)), dma(()), dma((4,)), dma((4,)), dma((3,)), dma((3,)),
            dma((4,)), dma((4,)), dma((2,)), dma((2,)),
            dma((8,)), dma((8,)), dma((4,)), dma((4,)), dma((4,)), dma((4,)),
            dma((8,)), dma((8,)), dma((8,)), dma((8,)),
        ],
        compiler_params=pltpu.CompilerParams(collective_id=1, has_side_effects=True, vmem_limit_bytes=LIMIT),
    )(send, part, pull, tokens, normed, grad, columns, signs, router, gain)


def local(tokens, norm_gain, router_w, w_gate, w_up, w_down, routes, grad_out):
    f32, bf16 = jnp.float32, jnp.bfloat16
    tok_dev, width = tokens.shape
    experts = lax.axis_size("expert")
    capacity = max(2, 3 * tok_dev * TOP // (2 * experts))
    tokens_wide = tokens.astype(f32)
    inverse = lax.rsqrt(jnp.mean(tokens_wide * tokens_wide, axis=1, keepdims=True) + 1e-06)
    unit_rows = tokens_wide * inverse
    normed = (unit_rows * norm_gain).astype(bf16)
    logits = jnp.dot(normed, router_w, preferred_element_type=f32)
    expert_ids = jnp.arange(experts, dtype=jnp.int32)[None, :]
    chosen = [routes[:, k : k + 1] == expert_ids for k in range(TOP)]
    picked = [jnp.sum(jnp.where(hot, logits, 0.0), axis=1) for hot in chosen]
    gate_pair = [jax.nn.sigmoid(picked[0] - picked[1]), jax.nn.sigmoid(picked[1] - picked[0])]

    token_ids = jnp.arange(tok_dev, dtype=jnp.int32)
    earlier = (token_ids[:, None] > token_ids[None, :]).astype(bf16)
    named = jnp.logical_or(chosen[0], chosen[1]).astype(bf16)
    ahead = jnp.dot(earlier, named, preferred_element_type=f32)
    slots = [
        routes[:, k] * (2 * capacity) + jnp.sum(jnp.where(chosen[k], ahead, 0.0), axis=1).astype(jnp.int32)
        for k in range(TOP)
    ]
    places = jnp.arange(experts * 2 * capacity, dtype=jnp.int32)
    hits = [places[:, None] == slot[None, :] for slot in slots]
    d_hits = [places[:, None] == slot[None, :] + capacity for slot in slots]
    pick = jnp.concatenate(
        [jnp.logical_or(hits[0], hits[1]).astype(bf16), jnp.logical_or(d_hits[0], d_hits[1]).astype(bf16)], axis=1
    )
    scale = jnp.sum(
        jnp.where(d_hits[0], gate_pair[0][None, :], 0.0) + jnp.where(d_hits[1], gate_pair[1][None, :], 0.0), axis=1
    )
    is_row = lax.rem(places, 2 * capacity) < capacity
    scale = jnp.where(is_row, 1.0, scale)
    stacked = jnp.concatenate([normed, grad_out], axis=0)
    send = (jnp.dot(pick, stacked, preferred_element_type=f32) * scale[:, None]).astype(bf16)
    arrived_both, gate_local, up_local, down_local = dispatch(
        send.reshape(experts, 2 * capacity, width), w_gate[0], w_up[0], w_down[0]
    )
    back, joined = expert(arrived_both, gate_local, up_local, down_local)
    part = joined.reshape(4, 4, 2, 2 * (width // lax.axis_size("dp")), joined.shape[1])
    hidden_units = w_gate.shape[2]
    pull = jnp.concatenate(
        [
            slots[0][:, None] == places[None, :],
            slots[1][:, None] == places[None, :],
            jnp.logical_or(
                slots[0][:, None] + capacity == places[None, :], slots[1][:, None] + capacity == places[None, :]
            ),
        ],
        axis=0,
    ).astype(bf16)
    columns = jnp.concatenate([inverse, gate_pair[0][:, None], gate_pair[1][:, None]], axis=1)
    signs = chosen[0].astype(f32) - chosen[1].astype(f32)
    layer_out, d_tokens, share, small = finish(
        back, part, pull, tokens, normed, grad_out, columns, signs, jnp.transpose(router_w), norm_gain[None, :]
    )
    return (
        layer_out,
        d_tokens,
        small[experts],
        jnp.transpose(small[:experts]),
        share[None, :, :hidden_units],
        share[None, :, hidden_units : 2 * hidden_units],
        jnp.transpose(share[:, 2 * hidden_units :])[None],
    )


def solution(mesh):
    rows, experts, copied = P(("dp", "expert"), None), P("expert", None, None), P()
    return jax.shard_map(
        local,
        mesh=mesh,
        in_specs=(rows, copied, copied, experts, experts, experts, rows, rows),
        out_specs=(
            rows,
            rows,
            copied,
            copied,
            P("expert", "dp", None),
            P("expert", "dp", None),
            P("expert", None, "dp"),
        ),
        check_vma=False,
    )
```
